32 devices in a mesh: gx: 8 (over z, core), gy: 4 (over y, x).
Axes of the slice: x: 2, y: 2, z: 4, core: 2. Of those that a mesh axis runs over, the one named last changes fastest.
Arguments:
- electric: float32 [3, 512, 128, 128], P(None, 'gx', 'gy'), may hold values from -6 to 6
- magnetic: float32 [3, 512, 128, 128], P(None, 'gx', 'gy'), may hold values from -6 to 6
- material_ids: int32 [512, 128, 128], P('gx', 'gy'), may hold values from 0 to 7
- inv_permittivity: float32 [8], replicated, may hold values from 0.08 to 1
- forward_field: bfloat16 [3, 3, 512, 128, 128], P(None, None, 'gx', 'gy'), may hold values from -6 to 6
- source_values: float32 [16384, 384], P(('gx', 'gy')), may hold values from -6 to 6
- source_tile: int32 [16384, 1], P(('gx', 'gy')), may hold values from 0 to 31; in each aligned block of 512 rows (0 to 511, 512 to 1023, ...) at most 32 rows name the same one
- source_cell: int32 [16384], P(('gx', 'gy')), may hold values from 0 to 2047
- owner_map: int32 [16], replicated, may hold values from 0 to 31, as said below
- shape_basis: float32 [128, 64, 64], replicated, may hold values from -0.09375 to 0.09375
Outputs:
- adjoint_e: float32 [3, 512, 128, 128], P(None, 'gx', 'gy')
- adjoint_h: float32 [3, 512, 128, 128], P(None, 'gx', 'gy')
- design_gradient: float32 [32, 128], P(('gx', 'gy'))
The draws below stay inside these ranges and needn't reach their ends.
Inputs may be any that keep to these rules, and one draw needn't show every extreme that they name: `source_tile`: each device's 512 source blocks name any one tile at most 32 times, a bound that some block reaches. `owner_map`: the owners of different design blocks are different devices; device 0 and the last device each own one.
All inputs are finite; a program needn't handle non-finite values.
Results may differ from the reference program's by a relative error of at most 0.0003.
Values sent between devices are 32-bit elements; how exact they have to be, the bound alone decides.
A program may use at most 128 MiB of HBM per device.

```python
import math
import jax
import jax.numpy as jnp
import numpy as np
from jax import lax

CX = 64
CY = 32
NZ = 128
STEPS = 3
MATERIALS = 8
BLOCK = 64
PARAMS = 128
SRC_DEV = 512
NX = 512
NY = 128
CAP = 32
BLOCKS_ALL = 16384
DESIGN_BLOCKS = 16
N_GX = 8
N_GY = 4
DEVICES = 32


def draw_owner_map(key, part):
    first_key = jax.random.fold_in(key, 11)
    second_key = jax.random.fold_in(key, 23)
    middle = jax.random.permutation(first_key, N_GX * N_GY - 2) + 1
    ends = jnp.array([0, N_GX * N_GY - 1], jnp.int32)
    chosen = jnp.concatenate([ends, middle[:DESIGN_BLOCKS - 2].astype(jnp.int32)])
    return jax.random.permutation(second_key, chosen).astype(jnp.int32)


def touch_ends(values, own_key, low, largest):
    longest = values.shape.index(max(values.shape))
    spots = []
    for shift in (0, 1):
        where = [jax.random.randint(jax.random.fold_in(own_key, axis), (), 0, length) for axis, length in enumerate(values.shape)]
        where[longest] = (where[longest] + shift) % values.shape[longest]
        spots.append(tuple(where))
    return values.at[spots[0]].set(low).at[spots[1]].set(largest)


def shard_levels(rng, extent, split, low, high):
    def one(position, blocks):
        steps = jax.random.uniform(jax.random.fold_in(jax.random.fold_in(rng, 6), position), (blocks,), jnp.float32, low / len(split), high / len(split))
        return jnp.repeat(jnp.exp(steps), extent[position] // blocks).reshape((-1,) + (1,) * (len(extent) - position - 1))

    level = one(*split[0])
    for cut in split[1:]:
        level = level * one(*cut)
    return level


def assign_block(stream_key, own, number, rows, amount, top, bound, slope):
    sequence = jax.random.permutation(stream_key, amount)
    heavy_load, usual = shares(amount, rows * top, bound, slope, True), shares(amount, rows * top, bound, slope, False)
    places = jnp.arange(amount)

    def named(tallies, offset_by):
        used = int((tallies > 0).sum())
        fixed = max(1, used // 4)
        shifted = fixed + (places - fixed + offset_by * (used - fixed)) % max(1, amount - fixed)
        return jnp.zeros((amount,), jnp.int32).at[sequence[jnp.where(places < fixed, places, shifted)]].set(jnp.asarray(tallies, jnp.int32))

    tallies = jnp.where(number % 4 == 0, named(heavy_load, number // 4), named(usual, number - number // 4 - 1))
    mixed = jax.random.permutation(jax.random.fold_in(own, 3), amount)
    donor, receiver = mixed[0:amount // 2 * 2:2], mixed[1:amount // 2 * 2:2]
    margin = jnp.minimum(tallies[donor] - 1, bound - tallies[receiver]) // 2
    margin = jnp.where((donor == sequence[0]) | (receiver == sequence[0]) | (tallies[receiver] == 0), 0, jnp.maximum(margin, 0))
    shifted = jax.random.randint(jax.random.fold_in(own, 4), (amount // 2,), 0, 1 << 20) % (margin + 1)
    tallies = tallies.at[donor].add(-shifted).at[receiver].add(shifted)
    members = jnp.searchsorted(jnp.cumsum(tallies), jnp.arange(rows * top), side="right").astype(jnp.int32)
    listing = members.reshape(top, rows).T
    listing = listing[jax.random.permutation(jax.random.fold_in(own, 1), rows)]
    offset_by = jax.random.randint(jax.random.fold_in(own, 2), (rows, 1), 0, top)
    return jnp.take_along_axis(listing, (jnp.arange(top)[None, :] + offset_by) % top, axis=1)


def shares(count, total, limit, skew, full):
    loads = [(1 << 20) // math.isqrt(grade ** skew) + 1 for grade in range(1, count + 1)]
    largest = limit if full else min(limit, max(-(-total // count), total * loads[0] // sum(loads)))
    least = 1 if total - largest >= count - 1 else 0
    given, spare = [largest] + [least] * (count - 1), total - largest - least * (count - 1)
    while spare > 0:
        free = [i for i in range(1, count) if given[i] < largest] or [i for i in range(1, count) if given[i] < limit]
        whole, budget = sum([loads[i] for i in free]), spare
        for i in free:
            addition = min(limit - given[i], max(1, budget * loads[i] // whole), spare)
            given[i] = given[i] + addition
            spare = spare - addition
    return np.array(given)


def normal_values(own_key, dims, spread, reach, cuts=(), kind=jnp.bfloat16):
    entries = spread * jax.random.normal(own_key, dims, jnp.float32)
    if cuts:
        entries = entries * shard_levels(own_key, dims, cuts, -0.22, 0.18)
    return jnp.clip(entries, -reach, reach).astype(kind)


def setup_inputs(seed: int = 0) -> dict:
    key_of = jax.random.split(jax.random.key(seed), 11)
    electric = normal_values(key_of[0], (3, NX, NY, NZ), 1.0, 6.0, ((1, 8), (2, 4)), jnp.float32)
    magnetic = normal_values(key_of[1], (3, NX, NY, NZ), 1.0, 6.0, ((1, 8), (2, 4)), jnp.float32)
    material_ids = touch_ends(jax.random.randint(key_of[2], (NX, NY, NZ), 0, MATERIALS), jax.random.fold_in(key_of[2], 1), 0, MATERIALS - 1).astype(jnp.int32)
    inv_permittivity = jnp.clip(jnp.exp(jax.random.uniform(key_of[3], (MATERIALS,), jnp.float32, math.log(0.08), math.log(1.0))), 0.08, 1.0)
    forward_field = normal_values(key_of[4], (STEPS, 3, NX, NY, NZ), 1.0, 6.0, ((2, 8), (3, 4)))
    source_values = normal_values(key_of[5], (BLOCKS_ALL, STEPS * NZ), 1.0, 6.0, ((0, 32),), jnp.float32)
    source_tile_keys = jax.random.split(jax.random.fold_in(key_of[6], 1), BLOCKS_ALL // SRC_DEV)
    source_tile_turns = jax.random.permutation(jax.random.fold_in(key_of[6], 3), BLOCKS_ALL // SRC_DEV)
    source_tile = jax.vmap(lambda own, number: assign_block(jax.random.fold_in(key_of[6], 2), own, number, SRC_DEV, DEVICES, 1, CAP, 2))(source_tile_keys, source_tile_turns).reshape((BLOCKS_ALL, 1))
    source_cell = touch_ends(jax.random.randint(key_of[7], (BLOCKS_ALL,), 0, CX * CY), jax.random.fold_in(key_of[7], 1), 0, (CX * CY) - 1).astype(jnp.int32)
    owner_map = draw_owner_map(jax.random.fold_in(key_of[10], 71), 0)
    shape_basis = normal_values(key_of[9], (PARAMS, BLOCK, BLOCK), (BLOCK * BLOCK) ** -0.5, 0.09375, (), jnp.float32)
    return {"electric": electric, "magnetic": magnetic, "material_ids": material_ids, "inv_permittivity": inv_permittivity, "forward_field": forward_field, "source_values": source_values, "source_tile": source_tile, "source_cell": source_cell, "owner_map": owner_map, "shape_basis": shape_basis}


time_step = 0.5
corr_scale = 0.0625


def plus_one(a, axis):
    rest = lax.slice_in_dim(a, 1, a.shape[axis], axis=axis)
    edge = jnp.zeros_like(lax.slice_in_dim(a, 0, 1, axis=axis))
    return jnp.concatenate([rest, edge], axis=axis)


def minus_one(a, axis):
    rest = lax.slice_in_dim(a, 0, a.shape[axis] - 1, axis=axis)
    edge = jnp.zeros_like(lax.slice_in_dim(a, 0, 1, axis=axis))
    return jnp.concatenate([edge, rest], axis=axis)


def reference(electric, magnetic, material_ids, inv_permittivity, forward_field, source_values, source_tile, source_cell, owner_map, shape_basis):
    inv_eps = jnp.zeros(material_ids.shape, jnp.float32)
    for mat in range(MATERIALS):
        inv_eps = inv_eps + jnp.where(material_ids == mat, inv_permittivity[mat], jnp.zeros((), inv_permittivity.dtype))
    target = source_tile[:, 0]
    col_x = (target // N_GY) * CX + source_cell // CY
    col_y = (target % N_GY) * CY + source_cell % CY
    corr = jnp.zeros((NX, NY), jnp.float32)
    for step in range(STEPS):
        ex, ey, ez = electric[0], electric[1], electric[2]
        curl_x = (plus_one(ez, 1) - ez) - (plus_one(ey, 2) - ey)
        curl_y = (plus_one(ex, 2) - ex) - (plus_one(ez, 0) - ez)
        curl_z = (plus_one(ey, 0) - ey) - (plus_one(ex, 1) - ex)
        magnetic = magnetic - time_step * jnp.stack([curl_x, curl_y, curl_z])
        hx, hy, hz = magnetic[0], magnetic[1], magnetic[2]
        drive = jnp.zeros((NX, NY, NZ), jnp.float32).at[col_x, col_y].add(source_values[:, step * NZ:(step + 1) * NZ])
        back_x = (hz - minus_one(hz, 1)) - (hy - minus_one(hy, 2))
        back_y = (hx - minus_one(hx, 2)) - (hz - minus_one(hz, 0))
        back_z = (hy - minus_one(hy, 0)) - (hx - minus_one(hx, 1)) - drive
        electric = electric + time_step * inv_eps * jnp.stack([back_x, back_y, back_z])
        corr = corr + jnp.sum(forward_field[step].astype(jnp.float32) * electric, axis=(0, 3))
    corr = corr * corr_scale
    blocks = corr.reshape(NX // BLOCK, BLOCK, NY // BLOCK, BLOCK).transpose(0, 2, 1, 3).reshape(DESIGN_BLOCKS, BLOCK * BLOCK)
    grads = jnp.dot(blocks, shape_basis.reshape(PARAMS, BLOCK * BLOCK).T, preferred_element_type=jnp.float32, precision=lax.Precision.HIGHEST)
    design_gradient = jnp.zeros((N_GX * N_GY, PARAMS), jnp.float32).at[owner_map].set(grads)
    return electric, magnetic, design_gradient
```

```python
import functools

import jax
import jax.numpy as jnp
from jax import lax
from jax.experimental import pallas as pl
from jax.experimental.pallas import tpu as pltpu
from jax.sharding import PartitionSpec as P

time_step = 0.5
corr_scale = 0.0625
PLANES = 4
MESH = pl.DeviceIdType.MESH


def split_bf16(value):
    high = value.astype(jnp.bfloat16)
    low = (value - high.astype(jnp.float32)).astype(jnp.bfloat16)
    return high, low


def kernel(
    grid_x,
    grid_y,
    tile_col,
    tile_row,
    cell_row,
    table,
    owners,
    values_hbm,
    electric_hbm,
    magnetic_hbm,
    ids_hbm,
    forward_hbm,
    basis_hbm,
    electric_out,
    magnetic_out,
    grad_out,
    values,
    e,
    h,
    ids,
    forward,
    basis,
    half_eps,
    acc,
    drive,
    one_hot,
    pack_hot,
    packed,
    got,
    cells_out,
    cells_got,
    cell_rows,
    halves,
    ex_out,
    ey_out,
    hx_out,
    hy_out,
    ex_in,
    ey_in,
    hx_in,
    hy_in,
    grad_send,
    grad_got,
    load_sem,
    store_sem,
    bulk_send,
    bulk_recv,
    halo_send,
    halo_recv,
):
    n = grid_x * grid_y
    width_x, width_y, depth = ids.shape
    steps = forward.shape[0]
    count = values.shape[0]
    rows = packed.shape[1]
    cap = rows // n
    per_lane = 128 // cap
    cell_total = width_x * width_y
    index_x = lax.axis_index("gx")
    index_y = lax.axis_index("gy")
    me = index_x * grid_y + index_y

    def place(device):
        return (device // grid_y, lax.rem(device, grid_y))

    def others(body):
        def step(k, carry):
            body(lax.rem(me + k, n))
            return carry

        lax.fori_loop(1, n, step, 0)

    barrier = pltpu.get_barrier_semaphore()

    def greet(device):
        pl.semaphore_signal(barrier, inc=1, device_id=place(device), device_id_type=MESH)

    others(greet)

    e_own = e.at[:, pl.ds(0, width_x)]
    h_own = h.at[:, pl.ds(1, width_x)]
    loads = [
        pltpu.make_async_copy(source, dest, load_sem.at[i])
        for i, (source, dest) in enumerate(
            [
                (values_hbm, values),
                (electric_hbm, e_own),
                (magnetic_hbm, h_own),
                (ids_hbm, ids),
                (forward_hbm, forward),
                (basis_hbm, basis),
            ]
        )
    ]
    for load in loads:
        load.start()

    trow = tile_row[...]
    same = (tile_col[...] == trow) & (
        lax.broadcasted_iota(jnp.int32, (count, count), 0)
        < lax.broadcasted_iota(jnp.int32, (count, count), 1)
    )
    slot = jnp.sum(jnp.where(same, 1.0, 0.0), axis=0, keepdims=True).astype(jnp.int32)
    dest = trow * cap + slot
    chunk = min(256, rows)

    def fill_pack(i, carry):
        start = pl.multiple_of(i * chunk, chunk)
        row = start + lax.broadcasted_iota(jnp.int32, (chunk, count), 0)
        pack_hot[pl.ds(start, chunk), :] = jnp.where(row == dest, 1.0, 0.0).astype(jnp.bfloat16)
        return carry

    lax.fori_loop(0, rows // chunk, fill_pack, 0)

    cell = cell_row[...] + 1
    lane_slot = slot + lax.rem(me, per_lane) * cap
    slot_hot = jnp.where(
        lax.broadcasted_iota(jnp.int32, (128, count), 0) == lane_slot, 1.0, 0.0
    ).astype(jnp.bfloat16)
    for_tile = lax.broadcasted_iota(jnp.int32, (n * 8, count), 0) // 8 == trow
    cell_high = jnp.where(for_tile, (cell // 64).astype(jnp.float32), 0.0).astype(jnp.bfloat16)
    cell_low = jnp.where(for_tile, lax.rem(cell, 64).astype(jnp.float32), 0.0).astype(jnp.bfloat16)
    lanes = (((1,), (1,)), ((), ()))
    sent_cells = 64.0 * lax.dot_general(
        cell_high, slot_hot, lanes, preferred_element_type=jnp.float32
    ) + lax.dot_general(cell_low, slot_hot, lanes, preferred_element_type=jnp.float32)
    cells_out[...] = sent_cells.reshape(n, 8, 128)
    cells_got[me] = cells_out[me]

    loads[0].wait()

    def pack(step):
        high, low = split_bf16(values[:, step * depth : (step + 1) * depth])
        both = jnp.concatenate([high, low], axis=1)

        def body(i, carry):
            start = pl.multiple_of(i * chunk, chunk)
            part = jnp.dot(
                pack_hot[pl.ds(start, chunk), :], both, preferred_element_type=jnp.float32
            )
            packed[step, pl.ds(start, chunk), :] = part[:, :depth] + part[:, depth:]
            return carry

        lax.fori_loop(0, rows // chunk, body, 0)
        mine = pl.ds(pl.multiple_of(me * cap, cap), cap)
        got[step, mine, :] = packed[step, mine, :]

    def send_values(step):
        mine = pl.ds(pl.multiple_of(me * cap, cap), cap)

        def send(device):
            pltpu.make_async_remote_copy(
                src_ref=packed.at[step, pl.ds(pl.multiple_of(device * cap, cap), cap)],
                dst_ref=got.at[step, mine],
                send_sem=bulk_send.at[step],
                recv_sem=bulk_recv.at[step],
                device_id=place(device),
                device_id_type=MESH,
            ).start()

        others(send)

    def wait_values(step, sem):
        part = got.at[step, pl.ds(0, (n - 1) * cap)]
        pltpu.make_async_copy(part, part, sem.at[step]).wait()

    def send_blocks(source, target, number):
        def send(device):
            pltpu.make_async_remote_copy(
                src_ref=source(device),
                dst_ref=target.at[me],
                send_sem=bulk_send.at[number],
                recv_sem=bulk_recv.at[number],
                device_id=place(device),
                device_id_type=MESH,
            ).start()

        others(send)

    def wait_blocks(target, sem, number):
        part = target.at[pl.ds(0, n - 1)]
        pltpu.make_async_copy(part, part, sem.at[number]).wait()

    pack(0)

    first_x = index_x == 0
    last_x = index_x == grid_x - 1
    first_y = index_y == 0
    last_y = index_y == grid_y - 1

    @pl.when(last_x)
    def _():
        ex_in[...] = jnp.zeros_like(ex_in)

    @pl.when(last_y)
    def _():
        ey_in[...] = jnp.zeros_like(ey_in)

    @pl.when(first_x)
    def _():
        hx_in[...] = jnp.zeros_like(hx_in)

    @pl.when(first_y)
    def _():
        hy_in[...] = jnp.zeros_like(hy_in)

    def halo(number, step, source, target, device):
        return pltpu.make_async_remote_copy(
            src_ref=source.at[step],
            dst_ref=target.at[step],
            send_sem=halo_send.at[number, step],
            recv_sem=halo_recv.at[number, step],
            device_id=device,
            device_id_type=MESH,
        )

    down_x = (jnp.maximum(index_x - 1, 0), index_y)
    up_x = (jnp.minimum(index_x + 1, grid_x - 1), index_y)
    down_y = (index_x, jnp.maximum(index_y - 1, 0))
    up_y = (index_x, jnp.minimum(index_y + 1, grid_y - 1))
    halos = [
        (0, ex_out, ex_in, down_x, ~first_x, ~last_x),
        (1, ey_out, ey_in, down_y, ~first_y, ~last_y),
        (2, hx_out, hx_in, up_x, ~last_x, ~first_x),
        (3, hy_out, hy_in, up_y, ~last_y, ~first_y),
    ]

    def halo_start(which, step):
        number, source, target, device, sends, _ = halos[which]

        @pl.when(sends)
        def _():
            halo(number, step, source, target, device).start()

    def halo_arrived(which, step):
        number, source, target, device, _, receives = halos[which]

        @pl.when(receives)
        def _():
            halo(number, step, source, target, device).wait_recv()

    def halo_left(which, step):
        number, source, target, device, sends, _ = halos[which]

        @pl.when(sends)
        def _():
            halo(number, step, source, target, device).wait_send()

    loads[1].wait()

    def stage_e(i, carry):
        for k in range(PLANES):
            x = i * PLANES + k
            ey_out[0, 0, pl.ds(x, 1), :] = e[0, x, pl.ds(0, 1), :]
            ey_out[0, 1, pl.ds(x, 1), :] = e[2, x, pl.ds(0, 1), :]
        return carry

    lax.fori_loop(0, width_x // PLANES, stage_e, 0)
    ex_out[0] = e[1:3, 0]

    pl.semaphore_wait(barrier, n - 1)
    halo_start(0, 0)
    halo_start(1, 0)
    send_blocks(lambda device: cells_out.at[device], cells_got, steps)
    send_values(0)
    for step in range(1, steps):
        pack(step)

    loads[3].wait()
    scalars = [time_step * table[m] for m in range(table.shape[0])]

    def fill_eps(i, carry):
        part = pl.ds(i * PLANES, PLANES)
        which = ids[part]
        value = jnp.zeros(which.shape, jnp.float32)
        for m, scalar in enumerate(scalars):
            value = jnp.where(which == m, scalar, value)
        half_eps[part] = value
        acc[part] = jnp.zeros(which.shape, jnp.float32)
        return carry

    lax.fori_loop(0, width_x // PLANES, fill_eps, 0)

    plane = (width_y, depth)
    row_id = lax.broadcasted_iota(jnp.int32, plane, 0)
    lane_id = lax.broadcasted_iota(jnp.int32, plane, 1)
    row_last, row_first = row_id == width_y - 1, row_id == 0
    lane_last, lane_first = lane_id == depth - 1, lane_id == 0

    def next_y(v, edge):
        return jnp.where(row_last, edge, pltpu.roll(v, width_y - 1, 0))

    def prev_y(v, edge):
        return jnp.where(row_first, edge, pltpu.roll(v, 1, 0))

    def next_z(v):
        return jnp.where(lane_last, 0.0, pltpu.roll(v, depth - 1, 1))

    def prev_z(v):
        return jnp.where(lane_first, 0.0, pltpu.roll(v, 1, 1))

    def h_phase(step):
        halo_arrived(0, step)
        e[1:3, width_x] = ex_in[step]
        halo_arrived(1, step)

        def body(i, carry):
            done = []
            for k in range(PLANES):
                x = i * PLANES + k
                ex, ey, ez = e[0, x], e[1, x], e[2, x]
                ey_next, ez_next = e[1, x + 1], e[2, x + 1]
                ex_y = next_y(ex, ey_in[step, 0, pl.ds(x, 1), :])
                ez_y = next_y(ez, ey_in[step, 1, pl.ds(x, 1), :])
                curl_x = (ez_y - ez) - (next_z(ey) - ey)
                curl_y = (next_z(ex) - ex) - (ez_next - ez)
                curl_z = (ey_next - ey) - (ex_y - ex)
                done.append(
                    (
                        x,
                        h[0, x + 1] - time_step * curl_x,
                        h[1, x + 1] - time_step * curl_y,
                        h[2, x + 1] - time_step * curl_z,
                    )
                )
            for x, hx, hy, hz in done:
                h[0, x + 1] = hx
                h[1, x + 1] = hy
                h[2, x + 1] = hz
                hy_out[step, 0, pl.ds(x, 1), :] = hx[width_y - 1 :, :]
                hy_out[step, 1, pl.ds(x, 1), :] = hz[width_y - 1 :, :]
            return carry

        lax.fori_loop(0, width_x // PLANES, body, 0)
        hx_out[step] = h[1:3, width_x]
        halo_start(2, step)
        halo_start(3, step)

    def e_phase(step, first, last):
        def body(i, carry):
            done = []
            for k in range(PLANES):
                x = i * PLANES + k
                hx, hy, hz = h[0, x + 1], h[1, x + 1], h[2, x + 1]
                hy_prev, hz_prev = h[1, x], h[2, x]
                hx_y = prev_y(hx, hy_in[step, 0, pl.ds(x, 1), :])
                hz_y = prev_y(hz, hy_in[step, 1, pl.ds(x, 1), :])
                back_x = (hz - hz_y) - (hy - prev_z(hy))
                back_y = (hx - prev_z(hx)) - (hz - hz_prev)
                back_z = (hy - hy_prev) - (hx - hx_y) - drive[x]
                scale = half_eps[x]
                ex = e[0, x] + scale * back_x
                ey = e[1, x] + scale * back_y
                ez = e[2, x] + scale * back_z
                total = (
                    acc[x]
                    + forward[step, 0, x].astype(jnp.float32) * ex
                    + forward[step, 1, x].astype(jnp.float32) * ey
                    + forward[step, 2, x].astype(jnp.float32) * ez
                )
                done.append((x, ex, ey, ez, total))
            for x, ex, ey, ez, total in done:
                e[0, x] = ex
                e[1, x] = ey
                e[2, x] = ez
                acc[x] = total
                if step + 1 < steps:
                    ey_out[step + 1, 0, pl.ds(x, 1), :] = ex[:1, :]
                    ey_out[step + 1, 1, pl.ds(x, 1), :] = ez[:1, :]
            return carry

        lax.fori_loop(first // PLANES, last // PLANES, body, 0)

    tile_rows = min(256, cell_total)

    def make_drive(step):
        high, low = split_bf16(got[step])
        halves[:, :depth] = high
        halves[:, depth:] = low

        def body(i, carry):
            start = pl.multiple_of(i * tile_rows, tile_rows)
            part = jnp.dot(
                one_hot[pl.ds(start, tile_rows), :],
                halves[...],
                preferred_element_type=jnp.float32,
            )
            drive[pl.ds(i * (tile_rows // width_y), tile_rows // width_y)] = (
                part[:, :depth] + part[:, depth:]
            ).reshape(tile_rows // width_y, width_y, depth)
            return carry

        lax.fori_loop(0, cell_total // tile_rows, body, 0)

    loads[2].wait()
    stores = []
    for step in range(steps):
        h_phase(step)
        if step == 0:
            loads[4].wait()
            loads[5].wait()
        if step + 1 < steps:
            send_values(step + 1)
        else:
            store = pltpu.make_async_copy(h_own, magnetic_out, store_sem.at[0])
            store.start()
            stores.append(store)
        if step == 0:
            wait_blocks(cells_got, bulk_recv, steps)
            for group in range(rows // 128):
                total = cells_got[group * per_lane]
                for k in range(1, per_lane):
                    total = total + cells_got[group * per_lane + k]
                cell_rows[group] = total.astype(jnp.int32) - 1

            def fill_hot(i, carry):
                start = pl.multiple_of(i * tile_rows, tile_rows)
                cell_id = start + lax.broadcasted_iota(jnp.int32, (tile_rows, 128), 0)
                for group in range(rows // 128):
                    hit = cell_id == cell_rows[group, 0:1, :]
                    one_hot[pl.ds(start, tile_rows), group * 128 : (group + 1) * 128] = (
                        jnp.where(hit, 1.0, 0.0).astype(jnp.bfloat16)
                    )
                return carry

            lax.fori_loop(0, cell_total // tile_rows, fill_hot, 0)
        wait_values(step, bulk_recv)
        make_drive(step)
        halo_arrived(2, step)
        h_store_plane = hx_in[step]
        h[1:3, 0] = h_store_plane
        halo_arrived(3, step)
        if step + 1 < steps:
            e_phase(step, 0, width_x)
            ex_out[step + 1] = e[1:3, 0]
            halo_start(0, step + 1)
            halo_start(1, step + 1)
        else:
            parts = 4
            size = width_x // parts
            for part in range(parts):
                e_phase(step, part * size, (part + 1) * size)
                store = pltpu.make_async_copy(
                    e.at[:, pl.ds(part * size, size)],
                    electric_out.at[:, pl.ds(part * size, size)],
                    store_sem.at[1 + part],
                )
                store.start()
                stores.append(store)

    side = basis.shape[1]
    offset = lax.rem(index_y * width_y, side)
    at_lane = lax.broadcasted_iota(jnp.int32, (width_y, side), 1) == (
        lax.broadcasted_iota(jnp.int32, (width_y, side), 0) + offset
    )
    column = jnp.sum(acc[...], axis=2, keepdims=True) * corr_scale
    corr = jnp.sum(jnp.where(at_lane[None], column, 0.0), axis=1)
    params = basis.shape[0]
    group = 16
    pieces = []
    ones = jnp.ones((8, side), jnp.float32)
    for start in range(0, params, group):
        pieces.append(jnp.sum(basis[start : start + group] * corr[None], axis=1))
    weighted = jnp.concatenate(pieces, axis=0)
    grad_send[...] = lax.dot_general(
        ones,
        weighted,
        (((1,), (1,)), ((), ())),
        preferred_element_type=jnp.float32,
        precision=lax.Precision.HIGHEST,
    )
    grad_got[me] = grad_send[...]
    send_blocks(lambda device: grad_send, grad_got, steps + 1)
    wait_blocks(grad_got, bulk_recv, steps + 1)

    def add(source, total):
        x, y = source // grid_y, lax.rem(source, grid_y)
        block = (x * width_x // side) * (width_y * grid_y // side) + y * width_y // side
        return total + jnp.where(owners[block] == me, grad_got[source], 0.0)

    total = lax.fori_loop(0, n, add, jnp.zeros(grad_send.shape, jnp.float32))
    grad_out[...] = total[:1, :]

    for store in stores:
        store.wait()
    for step in range(steps):
        wait_values(step, bulk_send)
        for which in range(4):
            halo_left(which, step)
    wait_blocks(cells_got, bulk_send, steps)
    wait_blocks(grad_got, bulk_send, steps + 1)


def per_device(
    electric,
    magnetic,
    material_ids,
    inv_permittivity,
    forward_field,
    source_values,
    source_tile,
    source_cell,
    owner_map,
    shape_basis,
):
    _, width_x, width_y, depth = electric.shape
    steps = forward_field.shape[0]
    grid_x = lax.axis_size("gx")
    grid_y = lax.axis_size("gy")
    n = grid_x * grid_y
    count = source_tile.shape[0]
    cap = max(2, 2 * count // n)
    rows = n * cap
    params = shape_basis.shape[0]
    f32, bf16 = jnp.float32, jnp.bfloat16
    vmem = pl.BlockSpec(memory_space=pltpu.VMEM)
    smem = pl.BlockSpec(memory_space=pltpu.SMEM)
    hbm = pl.BlockSpec(memory_space=pl.ANY)
    x_face = pltpu.VMEM((steps, 2, width_y, depth), f32)
    y_face = pltpu.VMEM((steps, 2, width_x, depth), f32)
    return pl.pallas_call(
        functools.partial(kernel, grid_x, grid_y),
        out_shape=(
            jax.ShapeDtypeStruct(electric.shape, f32),
            jax.ShapeDtypeStruct(magnetic.shape, f32),
            jax.ShapeDtypeStruct((1, params), f32),
        ),
        in_specs=[vmem, vmem, vmem, smem, smem] + [hbm] * 6,
        out_specs=(hbm, hbm, vmem),
        scratch_shapes=[
            pltpu.VMEM(source_values.shape, f32),
            pltpu.VMEM((3, width_x + 1, width_y, depth), f32),
            pltpu.VMEM((3, width_x + 1, width_y, depth), f32),
            pltpu.VMEM(material_ids.shape, jnp.int32),
            pltpu.VMEM(forward_field.shape, bf16),
            pltpu.VMEM(shape_basis.shape, f32),
            pltpu.VMEM(material_ids.shape, f32),
            pltpu.VMEM(material_ids.shape, f32),
            pltpu.VMEM(material_ids.shape, f32),
            pltpu.VMEM((width_x * width_y, rows), bf16),
            pltpu.VMEM((rows, count), bf16),
            pltpu.VMEM((steps, rows, depth), f32),
            pltpu.VMEM((steps, rows, depth), f32),
            pltpu.VMEM((n, 8, 128), f32),
            pltpu.VMEM((n, 8, 128), f32),
            pltpu.VMEM((rows // 128, 8, 128), jnp.int32),
            pltpu.VMEM((rows, 2 * depth), bf16),
            x_face,
            y_face,
            x_face,
            y_face,
            x_face,
            y_face,
            x_face,
            y_face,
            pltpu.VMEM((8, params), f32),
            pltpu.VMEM((n, 8, params), f32),
            pltpu.SemaphoreType.DMA((6,)),
            pltpu.SemaphoreType.DMA((5,)),
            pltpu.SemaphoreType.DMA((steps + 2,)),
            pltpu.SemaphoreType.DMA((steps + 2,)),
            pltpu.SemaphoreType.DMA((4, steps)),
            pltpu.SemaphoreType.DMA((4, steps)),
        ],
        compiler_params=pltpu.CompilerParams(
            collective_id=0, has_side_effects=True, vmem_limit_bytes=50 * 1024 * 1024
        ),
    )(
        source_tile,
        source_tile.reshape(1, count),
        source_cell.reshape(1, count),
        inv_permittivity,
        owner_map,
        source_values,
        electric,
        magnetic,
        material_ids,
        forward_field,
        shape_basis,
    )


def solution(mesh):
    placed = (
        P(None, "gx", "gy", None),
        P(None, "gx", "gy", None),
        P("gx", "gy", None),
        P(),
        P(None, None, "gx", "gy", None),
        P(("gx", "gy"), None),
        P(("gx", "gy"), None),
        P(("gx", "gy")),
        P(),
        P(),
    )
    return jax.shard_map(
        per_device,
        mesh=mesh,
        in_specs=placed,
        out_specs=(P(None, "gx", "gy", None), P(None, "gx", "gy", None), P(("gx", "gy"), None)),
        check_vma=False,
    )
```

```python
import functools

import jax
import jax.numpy as jnp
from jax import lax
from jax.experimental import pallas as pl
from jax.experimental.pallas import tpu as pltpu
from jax.sharding import PartitionSpec as P

time_step = 0.5
corr_scale = 0.0625
PLANES = 4
MESH = pl.DeviceIdType.MESH


def split_bf16(value):
    high = value.astype(jnp.bfloat16)
    low = (value - high.astype(jnp.float32)).astype(jnp.bfloat16)
    return high, low


def kernel(
    grid_x,
    grid_y,
    tile_row,
    cell_row,
    table,
    owners,
    values_hbm,
    electric_hbm,
    magnetic_hbm,
    ids_hbm,
    forward_hbm,
    basis_hbm,
    electric_out,
    magnetic_out,
    grad_out,
    values,
    e,
    h,
    ids,
    forward,
    basis,
    half_eps,
    acc,
    drive,
    one_hot,
    pack_hot,
    packed,
    got,
    cells_out,
    cells_got,
    cell_rows,
    halves,
    ex_out,
    ey_out,
    hx_out,
    hy_out,
    ex_in,
    ey_in,
    hx_in,
    hy_in,
    grad_send,
    grad_got,
    load_sem,
    store_sem,
    bulk_send,
    bulk_recv,
    halo_send,
    halo_recv,
):
    n = grid_x * grid_y
    width_x, width_y, depth = ids.shape
    steps = forward.shape[0]
    count = values.shape[0]
    rows = packed.shape[1]
    cap = rows // n
    per_lane = 128 // cap
    cell_total = width_x * width_y
    index_x = lax.axis_index("gx")
    index_y = lax.axis_index("gy")
    me = index_x * grid_y + index_y

    def others(body, first=0, last=grid_x):
        def one(kx, ky):
            x, y = index_x + kx, index_y + ky
            x = jnp.where(x >= grid_x, x - grid_x, x)
            y = jnp.where(y >= grid_y, y - grid_y, y)
            body(x * grid_y + y, (x, y))

        if first == 0:
            for ky in range(1, grid_y):
                one(0, ky)

        def step(kx, carry):
            for ky in range(grid_y):
                one(kx, ky)
            return carry

        lax.fori_loop(max(first, 1), last, step, 0)

    barrier = pltpu.get_barrier_semaphore()

    def greet(device, where):
        pl.semaphore_signal(barrier, inc=1, device_id=where, device_id_type=MESH)

    others(greet)

    side = basis_hbm.shape[0]
    offset = pl.multiple_of(lax.rem(index_y * width_y, side), width_y)
    e_own = e.at[:, pl.ds(0, width_x)]
    h_own = h.at[:, pl.ds(1, width_x)]
    loads = [
        pltpu.make_async_copy(source, dest, load_sem.at[i])
        for i, (source, dest) in enumerate(
            [
                (values_hbm, values),
                (electric_hbm, e_own),
                (magnetic_hbm, h_own),
                (ids_hbm, ids),
                (forward_hbm, forward),
                (basis_hbm.at[:, pl.ds(offset, width_y)], basis),
            ]
        )
    ]
    for load in loads:
        load.start()

    trow = tile_row[...]
    to_tile = lax.broadcasted_iota(jnp.int32, (n, count), 0) == trow
    earlier = lax.broadcasted_iota(jnp.int32, (count, count), 0) < (
        lax.broadcasted_iota(jnp.int32, (count, count), 1)
    )
    before = jnp.dot(
        jnp.where(to_tile, 1.0, 0.0).astype(jnp.bfloat16),
        jnp.where(earlier, 1.0, 0.0).astype(jnp.bfloat16),
        preferred_element_type=jnp.float32,
    )
    slot = jnp.sum(jnp.where(to_tile, before, 0.0), axis=0, keepdims=True).astype(jnp.int32)
    dest = trow * cap + slot
    chunk = min(256, rows)

    def fill_pack(i, carry):
        start = pl.multiple_of(i * chunk, chunk)
        row = start + lax.broadcasted_iota(jnp.int32, (chunk, count), 0)
        pack_hot[pl.ds(start, chunk), :] = jnp.where(row == dest, 1.0, 0.0).astype(jnp.bfloat16)
        return carry

    lax.fori_loop(0, rows // chunk, fill_pack, 0)

    cell = cell_row[...] + 1
    lane_slot = slot + lax.rem(me, per_lane) * cap
    slot_hot = jnp.where(
        lax.broadcasted_iota(jnp.int32, (128, count), 0) == lane_slot, 1.0, 0.0
    ).astype(jnp.bfloat16)
    for_tile = lax.broadcasted_iota(jnp.int32, (n * 8, count), 0) // 8 == trow
    cell_high = jnp.where(for_tile, (cell // 64).astype(jnp.float32), 0.0).astype(jnp.bfloat16)
    cell_low = jnp.where(for_tile, lax.rem(cell, 64).astype(jnp.float32), 0.0).astype(jnp.bfloat16)
    lanes = (((1,), (1,)), ((), ()))
    sent_cells = 64.0 * lax.dot_general(
        cell_high, slot_hot, lanes, preferred_element_type=jnp.float32
    ) + lax.dot_general(cell_low, slot_hot, lanes, preferred_element_type=jnp.float32)
    cells_out[...] = sent_cells.reshape(n, 8, 128)
    cells_got[me] = cells_out[me]

    loads[0].wait()

    def pack(step):
        high, low = split_bf16(values[:, step * depth : (step + 1) * depth])
        both = jnp.concatenate([high, low], axis=1)

        def body(i, carry):
            start = pl.multiple_of(i * chunk, chunk)
            part = jnp.dot(
                pack_hot[pl.ds(start, chunk), :], both, preferred_element_type=jnp.float32
            )
            packed[step, pl.ds(start, chunk), :] = part[:, :depth] + part[:, depth:]
            return carry

        lax.fori_loop(0, rows // chunk, body, 0)
        mine = pl.ds(pl.multiple_of(me * cap, cap), cap)
        got[step, mine, :] = packed[step, mine, :]

    def send_values(step, first=0, last=grid_x):
        mine = pl.ds(pl.multiple_of(me * cap, cap), cap)

        def send(device, where):
            pltpu.make_async_remote_copy(
                src_ref=packed.at[step, pl.ds(pl.multiple_of(device * cap, cap), cap)],
                dst_ref=got.at[step, mine],
                send_sem=bulk_send.at[step],
                recv_sem=bulk_recv.at[step],
                device_id=where,
                device_id_type=MESH,
            ).start()

        others(send, first, last)

    def wait_values(step, sem):
        part = got.at[step, pl.ds(0, (n - 1) * cap)]
        pltpu.make_async_copy(part, part, sem.at[step]).wait()

    def send_blocks(source, target, number):
        def send(device, where):
            pltpu.make_async_remote_copy(
                src_ref=source(device),
                dst_ref=target.at[me],
                send_sem=bulk_send.at[number],
                recv_sem=bulk_recv.at[number],
                device_id=where,
                device_id_type=MESH,
            ).start()

        others(send)

    def wait_blocks(target, sem, number):
        part = target.at[pl.ds(0, n - 1)]
        pltpu.make_async_copy(part, part, sem.at[number]).wait()

    pack(0)

    first_x = index_x == 0
    last_x = index_x == grid_x - 1
    first_y = index_y == 0
    last_y = index_y == grid_y - 1

    @pl.when(last_x)
    def _():
        ex_in[...] = jnp.zeros_like(ex_in)

    @pl.when(last_y)
    def _():
        ey_in[...] = jnp.zeros_like(ey_in)

    @pl.when(first_x)
    def _():
        hx_in[...] = jnp.zeros_like(hx_in)

    @pl.when(first_y)
    def _():
        hy_in[...] = jnp.zeros_like(hy_in)

    def halo(number, step, source, target, device):
        return pltpu.make_async_remote_copy(
            src_ref=source.at[step],
            dst_ref=target.at[step],
            send_sem=halo_send.at[number, step],
            recv_sem=halo_recv.at[number, step],
            device_id=device,
            device_id_type=MESH,
        )

    down_x = (jnp.maximum(index_x - 1, 0), index_y)
    up_x = (jnp.minimum(index_x + 1, grid_x - 1), index_y)
    down_y = (index_x, jnp.maximum(index_y - 1, 0))
    up_y = (index_x, jnp.minimum(index_y + 1, grid_y - 1))
    halos = [
        (0, ex_out, ex_in, down_x, ~first_x, ~last_x),
        (1, ey_out, ey_in, down_y, ~first_y, ~last_y),
        (2, hx_out, hx_in, up_x, ~last_x, ~first_x),
        (3, hy_out, hy_in, up_y, ~last_y, ~first_y),
    ]

    def halo_start(which, step):
        number, source, target, device, sends, _ = halos[which]

        @pl.when(sends)
        def _():
            halo(number, step, source, target, device).start()

    def halo_arrived(which, step):
        number, source, target, device, _, receives = halos[which]

        @pl.when(receives)
        def _():
            halo(number, step, source, target, device).wait_recv()

    def halo_left(which, step):
        number, source, target, device, sends, _ = halos[which]

        @pl.when(sends)
        def _():
            halo(number, step, source, target, device).wait_send()

    loads[1].wait()

    def stage_e(i, carry):
        for k in range(PLANES):
            x = i * PLANES + k
            ey_out[0, 0, pl.ds(x, 1), :] = e[0, x, pl.ds(0, 1), :]
            ey_out[0, 1, pl.ds(x, 1), :] = e[2, x, pl.ds(0, 1), :]
        return carry

    lax.fori_loop(0, width_x // PLANES, stage_e, 0)
    ex_out[0] = e[1:3, 0]

    pl.semaphore_wait(barrier, n - 1)
    halo_start(0, 0)
    halo_start(1, 0)
    send_blocks(lambda device: cells_out.at[device], cells_got, steps)
    send_values(0)
    for step in range(1, min(steps, 2)):
        pack(step)

    scalars = [time_step * table[m] for m in range(table.shape[0])]

    def fill_eps(i, carry):
        part = pl.ds(i * PLANES, PLANES)
        which = ids[part]
        value = jnp.zeros(which.shape, jnp.float32)
        for m, scalar in enumerate(scalars):
            value = jnp.where(which == m, scalar, value)
        half_eps[part] = value
        acc[part] = jnp.zeros(which.shape, jnp.float32)
        return carry

    plane = (width_y, depth)
    row_id = lax.broadcasted_iota(jnp.int32, plane, 0)
    lane_id = lax.broadcasted_iota(jnp.int32, plane, 1)
    row_last, row_first = row_id == width_y - 1, row_id == 0
    lane_last, lane_first = lane_id == depth - 1, lane_id == 0

    def next_y(v, edge):
        return jnp.where(row_last, edge, pltpu.roll(v, width_y - 1, 0))

    def prev_y(v, edge):
        return jnp.where(row_first, edge, pltpu.roll(v, 1, 0))

    def next_z(v):
        return jnp.where(lane_last, 0.0, pltpu.roll(v, depth - 1, 1))

    def prev_z(v):
        return jnp.where(lane_first, 0.0, pltpu.roll(v, 1, 1))

    def h_phase(step):
        halo_arrived(0, step)
        e[1:3, width_x] = ex_in[step]
        halo_arrived(1, step)

        def body(i, carry):
            done = []
            for k in range(PLANES):
                x = i * PLANES + k
                ex, ey, ez = e[0, x], e[1, x], e[2, x]
                ey_next, ez_next = e[1, x + 1], e[2, x + 1]
                ex_y = next_y(ex, ey_in[step, 0, pl.ds(x, 1), :])
                ez_y = next_y(ez, ey_in[step, 1, pl.ds(x, 1), :])
                curl_x = (ez_y - ez) - (next_z(ey) - ey)
                curl_y = (next_z(ex) - ex) - (ez_next - ez)
                curl_z = (ey_next - ey) - (ex_y - ex)
                done.append(
                    (
                        x,
                        h[0, x + 1] - time_step * curl_x,
                        h[1, x + 1] - time_step * curl_y,
                        h[2, x + 1] - time_step * curl_z,
                    )
                )
            for x, hx, hy, hz in done:
                h[0, x + 1] = hx
                h[1, x + 1] = hy
                h[2, x + 1] = hz
                hy_out[step, 0, pl.ds(x, 1), :] = hx[width_y - 1 :, :]
                hy_out[step, 1, pl.ds(x, 1), :] = hz[width_y - 1 :, :]
            return carry

        lax.fori_loop(0, width_x // PLANES, body, 0)
        hx_out[step] = h[1:3, width_x]
        halo_start(2, step)
        halo_start(3, step)

    def e_phase(step, first, last, carry_in):
        final = step + 1 == steps

        def body(i, carry):
            done = []
            for k in range(PLANES):
                x = i * PLANES + k
                hx, hy, hz = h[0, x + 1], h[1, x + 1], h[2, x + 1]
                hy_prev, hz_prev = h[1, x], h[2, x]
                hx_y = prev_y(hx, hy_in[step, 0, pl.ds(x, 1), :])
                hz_y = prev_y(hz, hy_in[step, 1, pl.ds(x, 1), :])
                back_x = (hz - hz_y) - (hy - prev_z(hy))
                back_y = (hx - prev_z(hx)) - (hz - hz_prev)
                back_z = (hy - hy_prev) - (hx - hx_y) - drive[x]
                scale = half_eps[x]
                ex = e[0, x] + scale * back_x
                ey = e[1, x] + scale * back_y
                ez = e[2, x] + scale * back_z
                total = (
                    acc[x]
                    + forward[step, 0, x].astype(jnp.float32) * ex
                    + forward[step, 1, x].astype(jnp.float32) * ey
                    + forward[step, 2, x].astype(jnp.float32) * ez
                )
                done.append((x, ex, ey, ez, total))
            for x, ex, ey, ez, total in done:
                e[0, x] = ex
                e[1, x] = ey
                e[2, x] = ez
                if final:
                    part = jnp.sum(total, axis=1, keepdims=True) * basis[x]
                    for y in range(0, width_y, 8):
                        carry = carry + part[y : y + 8]
                else:
                    acc[x] = total
                    ey_out[step + 1, 0, pl.ds(x, 1), :] = ex[:1, :]
                    ey_out[step + 1, 1, pl.ds(x, 1), :] = ez[:1, :]
            return carry

        return lax.fori_loop(first // PLANES, last // PLANES, body, carry_in)

    tile_rows = min(512, cell_total)

    def make_drive(step):
        high, low = split_bf16(got[step])
        halves[:, :depth] = high
        halves[:, depth:] = low

        def body(i, carry):
            start = pl.multiple_of(i * tile_rows, tile_rows)
            part = jnp.dot(
                one_hot[pl.ds(start, tile_rows), :],
                halves[...],
                preferred_element_type=jnp.float32,
            )
            drive[pl.ds(i * (tile_rows // width_y), tile_rows // width_y)] = (
                part[:, :depth] + part[:, depth:]
            ).reshape(tile_rows // width_y, width_y, depth)
            return carry

        lax.fori_loop(0, cell_total // tile_rows, body, 0)

    loads[2].wait()
    stores = []
    for step in range(steps):
        h_phase(step)
        if step == 0:
            if steps > 1:
                send_values(1)
            for later in range(2, steps):
                pack(later)
            loads[3].wait()
            lax.fori_loop(0, width_x // PLANES, fill_eps, 0)
            loads[4].wait()
            loads[5].wait()
        elif step + 1 < steps:
            send_values(step + 1, grid_x // 2, grid_x)
        if step + 1 == steps:
            store = pltpu.make_async_copy(h_own, magnetic_out, store_sem.at[0])
            store.start()
            stores.append(store)
        if step == 0:
            wait_blocks(cells_got, bulk_recv, steps)
            for group in range(rows // 128):
                total = cells_got[group * per_lane]
                for k in range(1, per_lane):
                    total = total + cells_got[group * per_lane + k]
                cell_rows[group] = total.astype(jnp.int32) - 1

            def fill_hot(i, carry):
                start = pl.multiple_of(i * tile_rows, tile_rows)
                cell_id = start + lax.broadcasted_iota(jnp.int32, (tile_rows, 128), 0)
                for group in range(rows // 128):
                    hit = cell_id == cell_rows[group, 0:1, :]
                    one_hot[pl.ds(start, tile_rows), group * 128 : (group + 1) * 128] = (
                        jnp.where(hit, 1.0, 0.0).astype(jnp.bfloat16)
                    )
                return carry

            lax.fori_loop(0, cell_total // tile_rows, fill_hot, 0)
        wait_values(step, bulk_recv)
        make_drive(step)
        halo_arrived(2, step)
        h_store_plane = hx_in[step]
        h[1:3, 0] = h_store_plane
        halo_arrived(3, step)
        if step + 1 < steps:
            e_phase(step, 0, width_x, 0)
            ex_out[step + 1] = e[1:3, 0]
            halo_start(0, step + 1)
            halo_start(1, step + 1)
            if step + 2 < steps:
                send_values(step + 2, 0, grid_x // 2)
        else:
            grad = jnp.zeros(grad_send.shape, jnp.float32)
            parts = 4
            size = width_x // parts
            for part in range(parts):
                grad = e_phase(step, part * size, (part + 1) * size, grad)
                store = pltpu.make_async_copy(
                    e.at[:, pl.ds(part * size, size)],
                    electric_out.at[:, pl.ds(part * size, size)],
                    store_sem.at[1 + part],
                )
                store.start()
                stores.append(store)

    grad_send[...] = grad * corr_scale
    grad_got[me] = grad_send[...]
    send_blocks(lambda device: grad_send, grad_got, steps + 1)
    wait_blocks(grad_got, bulk_recv, steps + 1)

    def add(source, total):
        x, y = source // grid_y, lax.rem(source, grid_y)
        block = (x * width_x // side) * (width_y * grid_y // side) + y * width_y // side
        return total + jnp.where(owners[block] == me, grad_got[source], 0.0)

    total = lax.fori_loop(0, n, add, jnp.zeros(grad_send.shape, jnp.float32))
    grad_out[...] = jnp.sum(total, axis=0, keepdims=True)

    for store in stores:
        store.wait()
    for step in range(steps):
        wait_values(step, bulk_send)
        for which in range(4):
            halo_left(which, step)
    wait_blocks(cells_got, bulk_send, steps)
    wait_blocks(grad_got, bulk_send, steps + 1)


def hand_over(electric, magnetic, grad, electric_out, magnetic_out, grad_out, sem):
    size = electric.shape[1] // 4
    copies = []
    for i, (source, dest) in enumerate([(electric, electric_out), (magnetic, magnetic_out)]):
        for c in range(3):
            for k in range(4):
                part = pl.ds(k * size, size)
                copies.append(
                    pltpu.make_async_copy(source.at[c, part], dest.at[c, part], sem.at[i, c, k])
                )
    for copy in copies:
        copy.start()
    grad_out[...] = grad[...]
    for copy in copies:
        copy.wait()


def per_device(
    electric,
    magnetic,
    material_ids,
    inv_permittivity,
    forward_field,
    source_values,
    source_tile,
    source_cell,
    owner_map,
    shape_basis,
):
    _, width_x, width_y, depth = electric.shape
    steps = forward_field.shape[0]
    grid_x = lax.axis_size("gx")
    grid_y = lax.axis_size("gy")
    n = grid_x * grid_y
    count = source_tile.shape[0]
    cap = max(2, 2 * count // n)
    rows = n * cap
    params = shape_basis.shape[0]
    f32, bf16 = jnp.float32, jnp.bfloat16
    vmem = pl.BlockSpec(memory_space=pltpu.VMEM)
    smem = pl.BlockSpec(memory_space=pltpu.SMEM)
    hbm = pl.BlockSpec(memory_space=pl.ANY)
    x_face = pltpu.VMEM((steps, 2, width_y, depth), f32)
    y_face = pltpu.VMEM((steps, 2, width_x, depth), f32)
    results = pl.pallas_call(
        functools.partial(kernel, grid_x, grid_y),
        out_shape=(
            jax.ShapeDtypeStruct(electric.shape, f32),
            jax.ShapeDtypeStruct(magnetic.shape, f32),
            jax.ShapeDtypeStruct((1, params), f32),
        ),
        in_specs=[vmem, vmem, smem, smem] + [hbm] * 6,
        out_specs=(hbm, hbm, vmem),
        scratch_shapes=[
            pltpu.VMEM(source_values.shape, f32),
            pltpu.VMEM((3, width_x + 1, width_y, depth), f32),
            pltpu.VMEM((3, width_x + 1, width_y, depth), f32),
            pltpu.VMEM(material_ids.shape, jnp.int32),
            pltpu.VMEM(forward_field.shape, bf16),
            pltpu.VMEM((width_x, width_y, params), f32),
            pltpu.VMEM(material_ids.shape, f32),
            pltpu.VMEM(material_ids.shape, f32),
            pltpu.VMEM(material_ids.shape, f32),
            pltpu.VMEM((width_x * width_y, rows), bf16),
            pltpu.VMEM((rows, count), bf16),
            pltpu.VMEM((steps, rows, depth), f32),
            pltpu.VMEM((steps, rows, depth), f32),
            pltpu.VMEM((n, 8, 128), f32),
            pltpu.VMEM((n, 8, 128), f32),
            pltpu.VMEM((rows // 128, 8, 128), jnp.int32),
            pltpu.VMEM((rows, 2 * depth), bf16),
            x_face,
            y_face,
            x_face,
            y_face,
            x_face,
            y_face,
            x_face,
            y_face,
            pltpu.VMEM((8, params), f32),
            pltpu.VMEM((n, 8, params), f32),
            pltpu.SemaphoreType.DMA((6,)),
            pltpu.SemaphoreType.DMA((5,)),
            pltpu.SemaphoreType.DMA((steps + 2,)),
            pltpu.SemaphoreType.DMA((steps + 2,)),
            pltpu.SemaphoreType.DMA((4, steps)),
            pltpu.SemaphoreType.DMA((4, steps)),
        ],
        compiler_params=pltpu.CompilerParams(
            collective_id=0, has_side_effects=True, vmem_limit_bytes=60 * 1024 * 1024
        ),
    )(
        source_tile.reshape(1, count),
        source_cell.reshape(1, count),
        inv_permittivity,
        owner_map,
        source_values,
        electric,
        magnetic,
        material_ids,
        forward_field,
        jnp.transpose(shape_basis, (1, 2, 0)),
    )
    return pl.pallas_call(
        hand_over,
        out_shape=tuple(jax.ShapeDtypeStruct(r.shape, r.dtype) for r in results),
        in_specs=[hbm, hbm, vmem],
        out_specs=(hbm, hbm, vmem),
        scratch_shapes=[pltpu.SemaphoreType.DMA((2, 3, 4))],
        compiler_params=pltpu.CompilerParams(vmem_limit_bytes=60 * 1024 * 1024),
    )(*results)


def solution(mesh):
    placed = (
        P(None, "gx", "gy", None),
        P(None, "gx", "gy", None),
        P("gx", "gy", None),
        P(),
        P(None, None, "gx", "gy", None),
        P(("gx", "gy"), None),
        P(("gx", "gy"), None),
        P(("gx", "gy")),
        P(),
        P(),
    )
    return jax.shard_map(
        per_device,
        mesh=mesh,
        in_specs=placed,
        out_specs=(P(None, "gx", "gy", None), P(None, "gx", "gy", None), P(("gx", "gy"), None)),
        check_vma=False,
    )
```

```python
import functools

import jax
import jax.numpy as jnp
from jax import lax
from jax.experimental import pallas as pl
from jax.experimental.pallas import tpu as pltpu
from jax.sharding import PartitionSpec as P

time_step = 0.5
corr_scale = 0.0625
PLANES = 4
MESH = pl.DeviceIdType.MESH


def split_bf16(value):
    high = value.astype(jnp.bfloat16)
    low = (value - high.astype(jnp.float32)).astype(jnp.bfloat16)
    return high, low


def kernel(
    grid_x,
    grid_y,
    tile_row,
    cell_row,
    table,
    owners,
    values_hbm,
    electric_hbm,
    magnetic_hbm,
    ids_hbm,
    forward_hbm,
    basis_hbm,
    electric_out,
    magnetic_out,
    grad_out,
    values,
    e,
    h,
    ids,
    forward,
    basis,
    half_eps,
    acc,
    drive,
    one_hot,
    pack_hot,
    packed,
    got,
    cells_out,
    cells_got,
    cell_rows,
    halves,
    ex_out,
    ey_out,
    hx_out,
    hy_out,
    ex_in,
    ey_in,
    hx_in,
    hy_in,
    grad_send,
    grad_got,
    load_sem,
    store_sem,
    bulk_send,
    bulk_recv,
    halo_send,
    halo_recv,
):
    n = grid_x * grid_y
    width_x, width_y, depth = ids.shape
    steps = forward.shape[0]
    count = values.shape[0]
    rows = packed.shape[1]
    cap = rows // n
    per_lane = 128 // cap
    cell_total = width_x * width_y
    index_x = lax.axis_index("gx")
    index_y = lax.axis_index("gy")
    me = index_x * grid_y + index_y

    def others(body, first=0, last=grid_x):
        def one(kx, ky):
            x, y = index_x + kx, index_y + ky
            x = jnp.where(x >= grid_x, x - grid_x, x)
            y = jnp.where(y >= grid_y, y - grid_y, y)
            body(x * grid_y + y, (x, y))

        def step(i, carry):
            kx = grid_x // 2 + (2 * lax.rem(i, 2) - 1) * ((i + 1) // 2)
            for ky in range(grid_y):
                one(kx, ky)
            return carry

        lax.fori_loop(first, min(last, grid_x - 1), step, 0)
        if last == grid_x:
            for ky in range(1, grid_y):
                one(0, ky)

    barrier = pltpu.get_barrier_semaphore()

    def greet(device, where):
        pl.semaphore_signal(barrier, inc=1, device_id=where, device_id_type=MESH)

    others(greet)

    side = basis_hbm.shape[0]
    offset = pl.multiple_of(lax.rem(index_y * width_y, side), width_y)
    e_own = e.at[:, pl.ds(0, width_x)]
    h_own = h.at[:, pl.ds(1, width_x)]
    loads = [
        pltpu.make_async_copy(source, dest, load_sem.at[i])
        for i, (source, dest) in enumerate(
            [
                (values_hbm, values),
                (electric_hbm, e_own),
                (magnetic_hbm, h_own),
                (ids_hbm, ids),
                (forward_hbm, forward),
                (basis_hbm.at[:, pl.ds(offset, width_y)], basis),
            ]
        )
    ]
    for load in loads:
        load.start()

    trow = tile_row[...]
    to_tile = lax.broadcasted_iota(jnp.int32, (n, count), 0) == trow
    earlier = lax.broadcasted_iota(jnp.int32, (count, count), 0) < (
        lax.broadcasted_iota(jnp.int32, (count, count), 1)
    )
    before = jnp.dot(
        jnp.where(to_tile, 1.0, 0.0).astype(jnp.bfloat16),
        jnp.where(earlier, 1.0, 0.0).astype(jnp.bfloat16),
        preferred_element_type=jnp.float32,
    )
    slot = jnp.sum(jnp.where(to_tile, before, 0.0), axis=0, keepdims=True).astype(jnp.int32)
    dest = trow * cap + slot
    chunk = min(256, rows)

    def fill_pack(i, carry):
        start = pl.multiple_of(i * chunk, chunk)
        row = start + lax.broadcasted_iota(jnp.int32, (chunk, count), 0)
        pack_hot[pl.ds(start, chunk), :] = jnp.where(row == dest, 1.0, 0.0).astype(jnp.bfloat16)
        return carry

    lax.fori_loop(0, rows // chunk, fill_pack, 0)

    cell = cell_row[...] + 1
    lane_slot = slot + lax.rem(me, per_lane) * cap
    slot_hot = jnp.where(
        lax.broadcasted_iota(jnp.int32, (128, count), 0) == lane_slot, 1.0, 0.0
    ).astype(jnp.bfloat16)
    for_tile = lax.broadcasted_iota(jnp.int32, (n * 8, count), 0) // 8 == trow
    cell_high = jnp.where(for_tile, (cell // 64).astype(jnp.float32), 0.0).astype(jnp.bfloat16)
    cell_low = jnp.where(for_tile, lax.rem(cell, 64).astype(jnp.float32), 0.0).astype(jnp.bfloat16)
    lanes = (((1,), (1,)), ((), ()))
    sent_cells = 64.0 * lax.dot_general(
        cell_high, slot_hot, lanes, preferred_element_type=jnp.float32
    ) + lax.dot_general(cell_low, slot_hot, lanes, preferred_element_type=jnp.float32)
    cells_out[...] = sent_cells.reshape(n, 8, 128)
    cells_got[me] = cells_out[me]

    loads[0].wait()

    def pack(step):
        high, low = split_bf16(values[:, step * depth : (step + 1) * depth])
        both = jnp.concatenate([high, low], axis=1)

        def body(i, carry):
            start = pl.multiple_of(i * chunk, chunk)
            part = jnp.dot(
                pack_hot[pl.ds(start, chunk), :], both, preferred_element_type=jnp.float32
            )
            packed[step, pl.ds(start, chunk), :] = part[:, :depth] + part[:, depth:]
            return carry

        lax.fori_loop(0, rows // chunk, body, 0)
        mine = pl.ds(pl.multiple_of(me * cap, cap), cap)
        got[step, mine, :] = packed[step, mine, :]

    def send_values(step, first=0, last=grid_x):
        mine = pl.ds(pl.multiple_of(me * cap, cap), cap)

        def send(device, where):
            pltpu.make_async_remote_copy(
                src_ref=packed.at[step, pl.ds(pl.multiple_of(device * cap, cap), cap)],
                dst_ref=got.at[step, mine],
                send_sem=bulk_send.at[step],
                recv_sem=bulk_recv.at[step],
                device_id=where,
                device_id_type=MESH,
            ).start()

        others(send, first, last)

    def wait_values(step, sem):
        part = got.at[step, pl.ds(0, (n - 1) * cap)]
        pltpu.make_async_copy(part, part, sem.at[step]).wait()

    def send_blocks(source, target, number):
        def send(device, where):
            pltpu.make_async_remote_copy(
                src_ref=source(device),
                dst_ref=target.at[me],
                send_sem=bulk_send.at[number],
                recv_sem=bulk_recv.at[number],
                device_id=where,
                device_id_type=MESH,
            ).start()

        others(send)

    def wait_blocks(target, sem, number):
        part = target.at[pl.ds(0, n - 1)]
        pltpu.make_async_copy(part, part, sem.at[number]).wait()

    pack(0)

    first_x = index_x == 0
    last_x = index_x == grid_x - 1
    first_y = index_y == 0
    last_y = index_y == grid_y - 1

    @pl.when(last_x)
    def _():
        ex_in[...] = jnp.zeros_like(ex_in)

    @pl.when(last_y)
    def _():
        ey_in[...] = jnp.zeros_like(ey_in)

    @pl.when(first_x)
    def _():
        hx_in[...] = jnp.zeros_like(hx_in)

    @pl.when(first_y)
    def _():
        hy_in[...] = jnp.zeros_like(hy_in)

    def halo(number, step, source, target, device):
        return pltpu.make_async_remote_copy(
            src_ref=source.at[step],
            dst_ref=target.at[step],
            send_sem=halo_send.at[number, step],
            recv_sem=halo_recv.at[number, step],
            device_id=device,
            device_id_type=MESH,
        )

    down_x = (jnp.maximum(index_x - 1, 0), index_y)
    up_x = (jnp.minimum(index_x + 1, grid_x - 1), index_y)
    down_y = (index_x, jnp.maximum(index_y - 1, 0))
    up_y = (index_x, jnp.minimum(index_y + 1, grid_y - 1))
    halos = [
        (0, ex_out, ex_in, down_x, ~first_x, ~last_x),
        (1, ey_out, ey_in, down_y, ~first_y, ~last_y),
        (2, hx_out, hx_in, up_x, ~last_x, ~first_x),
        (3, hy_out, hy_in, up_y, ~last_y, ~first_y),
    ]

    def halo_start(which, step):
        number, source, target, device, sends, _ = halos[which]

        @pl.when(sends)
        def _():
            halo(number, step, source, target, device).start()

    def halo_arrived(which, step):
        number, source, target, device, _, receives = halos[which]

        @pl.when(receives)
        def _():
            halo(number, step, source, target, device).wait_recv()

    def halo_left(which, step):
        number, source, target, device, sends, _ = halos[which]

        @pl.when(sends)
        def _():
            halo(number, step, source, target, device).wait_send()

    loads[1].wait()

    def stage_e(i, carry):
        for k in range(PLANES):
            x = i * PLANES + k
            ey_out[0, 0, pl.ds(x, 1), :] = e[0, x, pl.ds(0, 1), :]
            ey_out[0, 1, pl.ds(x, 1), :] = e[2, x, pl.ds(0, 1), :]
        return carry

    lax.fori_loop(0, width_x // PLANES, stage_e, 0)
    ex_out[0] = e[1:3, 0]

    pl.semaphore_wait(barrier, n - 1)
    halo_start(0, 0)
    halo_start(1, 0)
    send_blocks(lambda device: cells_out.at[device], cells_got, steps)
    send_values(0)
    for step in range(1, min(steps, 2)):
        pack(step)

    scalars = [time_step * table[m] for m in range(table.shape[0])]

    def fill_eps(i, carry):
        part = pl.ds(i * PLANES, PLANES)
        which = ids[part]
        value = jnp.zeros(which.shape, jnp.float32)
        for m, scalar in enumerate(scalars):
            value = jnp.where(which == m, scalar, value)
        half_eps[part] = value
        acc[part] = jnp.zeros(which.shape, jnp.float32)
        return carry

    plane = (width_y, depth)
    row_id = lax.broadcasted_iota(jnp.int32, plane, 0)
    lane_id = lax.broadcasted_iota(jnp.int32, plane, 1)
    row_last, row_first = row_id == width_y - 1, row_id == 0
    lane_last, lane_first = lane_id == depth - 1, lane_id == 0

    def next_y(v, edge):
        return jnp.where(row_last, edge, pltpu.roll(v, width_y - 1, 0))

    def prev_y(v, edge):
        return jnp.where(row_first, edge, pltpu.roll(v, 1, 0))

    def next_z(v):
        return jnp.where(lane_last, 0.0, pltpu.roll(v, depth - 1, 1))

    def prev_z(v):
        return jnp.where(lane_first, 0.0, pltpu.roll(v, 1, 1))

    def h_phase(step):
        halo_arrived(0, step)
        e[1:3, width_x] = ex_in[step]
        halo_arrived(1, step)

        def body(i, carry):
            done = []
            for k in range(PLANES):
                x = i * PLANES + k
                ex, ey, ez = e[0, x], e[1, x], e[2, x]
                ey_next, ez_next = e[1, x + 1], e[2, x + 1]
                ex_y = next_y(ex, ey_in[step, 0, pl.ds(x, 1), :])
                ez_y = next_y(ez, ey_in[step, 1, pl.ds(x, 1), :])
                curl_x = (ez_y - ez) - (next_z(ey) - ey)
                curl_y = (next_z(ex) - ex) - (ez_next - ez)
                curl_z = (ey_next - ey) - (ex_y - ex)
                done.append(
                    (
                        x,
                        h[0, x + 1] - time_step * curl_x,
                        h[1, x + 1] - time_step * curl_y,
                        h[2, x + 1] - time_step * curl_z,
                    )
                )
            for x, hx, hy, hz in done:
                h[0, x + 1] = hx
                h[1, x + 1] = hy
                h[2, x + 1] = hz
                hy_out[step, 0, pl.ds(x, 1), :] = hx[width_y - 1 :, :]
                hy_out[step, 1, pl.ds(x, 1), :] = hz[width_y - 1 :, :]
            return carry

        lax.fori_loop(0, width_x // PLANES, body, 0)
        hx_out[step] = h[1:3, width_x]
        halo_start(2, step)
        halo_start(3, step)

    def e_phase(step, first, last, carry_in):
        final = step + 1 == steps

        def body(i, carry):
            done = []
            for k in range(PLANES):
                x = i * PLANES + k
                hx, hy, hz = h[0, x + 1], h[1, x + 1], h[2, x + 1]
                hy_prev, hz_prev = h[1, x], h[2, x]
                hx_y = prev_y(hx, hy_in[step, 0, pl.ds(x, 1), :])
                hz_y = prev_y(hz, hy_in[step, 1, pl.ds(x, 1), :])
                back_x = (hz - hz_y) - (hy - prev_z(hy))
                back_y = (hx - prev_z(hx)) - (hz - hz_prev)
                back_z = (hy - hy_prev) - (hx - hx_y) - drive[x]
                scale = half_eps[x]
                ex = e[0, x] + scale * back_x
                ey = e[1, x] + scale * back_y
                ez = e[2, x] + scale * back_z
                total = (
                    acc[x]
                    + forward[step, 0, x].astype(jnp.float32) * ex
                    + forward[step, 1, x].astype(jnp.float32) * ey
                    + forward[step, 2, x].astype(jnp.float32) * ez
                )
                done.append((x, ex, ey, ez, total))
            for x, ex, ey, ez, total in done:
                e[0, x] = ex
                e[1, x] = ey
                e[2, x] = ez
                if final:
                    part = jnp.sum(total, axis=1, keepdims=True) * basis[x]
                    for y in range(0, width_y, 8):
                        carry = carry + part[y : y + 8]
                else:
                    acc[x] = total
                    ey_out[step + 1, 0, pl.ds(x, 1), :] = ex[:1, :]
                    ey_out[step + 1, 1, pl.ds(x, 1), :] = ez[:1, :]
            return carry

        return lax.fori_loop(first // PLANES, last // PLANES, body, carry_in)

    tile_rows = min(512, cell_total)

    def make_drive(step):
        high, low = split_bf16(got[step])
        halves[:, :depth] = high
        halves[:, depth:] = low

        def body(i, carry):
            start = pl.multiple_of(i * tile_rows, tile_rows)
            part = jnp.dot(
                one_hot[pl.ds(start, tile_rows), :],
                halves[...],
                preferred_element_type=jnp.float32,
            )
            drive[pl.ds(i * (tile_rows // width_y), tile_rows // width_y)] = (
                part[:, :depth] + part[:, depth:]
            ).reshape(tile_rows // width_y, width_y, depth)
            return carry

        lax.fori_loop(0, cell_total // tile_rows, body, 0)

    loads[2].wait()
    stores = []
    for step in range(steps):
        h_phase(step)
        if step == 0:
            if steps > 1:
                send_values(1)
            for later in range(2, steps):
                pack(later)
            loads[3].wait()
            lax.fori_loop(0, width_x // PLANES, fill_eps, 0)
            loads[4].wait()
            loads[5].wait()
        elif step + 1 < steps:
            send_values(step + 1, grid_x // 2, grid_x)
        if step + 1 == steps:
            store = pltpu.make_async_copy(h_own, magnetic_out, store_sem.at[0])
            store.start()
            stores.append(store)
        if step == 0:
            wait_blocks(cells_got, bulk_recv, steps)
            for group in range(rows // 128):
                total = cells_got[group * per_lane]
                for k in range(1, per_lane):
                    total = total + cells_got[group * per_lane + k]
                cell_rows[group] = total.astype(jnp.int32) - 1

            def fill_hot(i, carry):
                start = pl.multiple_of(i * tile_rows, tile_rows)
                cell_id = start + lax.broadcasted_iota(jnp.int32, (tile_rows, 128), 0)
                for group in range(rows // 128):
                    hit = cell_id == cell_rows[group, 0:1, :]
                    one_hot[pl.ds(start, tile_rows), group * 128 : (group + 1) * 128] = (
                        jnp.where(hit, 1.0, 0.0).astype(jnp.bfloat16)
                    )
                return carry

            lax.fori_loop(0, cell_total // tile_rows, fill_hot, 0)
        wait_values(step, bulk_recv)
        make_drive(step)
        halo_arrived(2, step)
        h_store_plane = hx_in[step]
        h[1:3, 0] = h_store_plane
        halo_arrived(3, step)
        if step + 1 < steps:
            e_phase(step, 0, width_x, 0)
            ex_out[step + 1] = e[1:3, 0]
            halo_start(0, step + 1)
            halo_start(1, step + 1)
            if step + 2 < steps:
                send_values(step + 2, 0, grid_x // 2)
        else:
            grad = jnp.zeros(grad_send.shape, jnp.float32)
            parts = 4
            size = width_x // parts
            for part in range(parts):
                grad = e_phase(step, part * size, (part + 1) * size, grad)
                store = pltpu.make_async_copy(
                    e.at[:, pl.ds(part * size, size)],
                    electric_out.at[:, pl.ds(part * size, size)],
                    store_sem.at[1 + part],
                )
                store.start()
                stores.append(store)

    grad_send[...] = grad * corr_scale
    grad_got[me] = grad_send[...]
    send_blocks(lambda device: grad_send, grad_got, steps + 1)
    wait_blocks(grad_got, bulk_recv, steps + 1)

    def add(source, total):
        x, y = source // grid_y, lax.rem(source, grid_y)
        block = (x * width_x // side) * (width_y * grid_y // side) + y * width_y // side
        return total + jnp.where(owners[block] == me, grad_got[source], 0.0)

    total = lax.fori_loop(0, n, add, jnp.zeros(grad_send.shape, jnp.float32))
    grad_out[...] = jnp.sum(total, axis=0, keepdims=True)

    for store in stores:
        store.wait()
    for step in range(steps):
        wait_values(step, bulk_send)
        for which in range(4):
            halo_left(which, step)
    wait_blocks(cells_got, bulk_send, steps)
    wait_blocks(grad_got, bulk_send, steps + 1)


def hand_over(
    electric, magnetic, grad, electric_out, magnetic_out, grad_out, held_e, held_h, in_sem, out_sem
):
    size = electric.shape[1] // 4
    copies = []
    arrays = [(electric, held_e, electric_out), (magnetic, held_h, magnetic_out)]
    for i, (source, held, dest) in enumerate(arrays):
        for c in range(3):
            for k in range(4):
                part = pl.ds(k * size, size)
                copies.append(
                    (
                        pltpu.make_async_copy(
                            source.at[c, part], held.at[c, part], in_sem.at[i, c, k]
                        ),
                        pltpu.make_async_copy(
                            held.at[c, part], dest.at[c, part], out_sem.at[i, c, k]
                        ),
                    )
                )
    for load, _ in copies:
        load.start()
    grad_out[...] = grad[...]
    for load, store in copies:
        load.wait()
        store.start()
    for _, store in copies:
        store.wait()


def per_device(
    electric,
    magnetic,
    material_ids,
    inv_permittivity,
    forward_field,
    source_values,
    source_tile,
    source_cell,
    owner_map,
    shape_basis,
):
    _, width_x, width_y, depth = electric.shape
    steps = forward_field.shape[0]
    grid_x = lax.axis_size("gx")
    grid_y = lax.axis_size("gy")
    n = grid_x * grid_y
    count = source_tile.shape[0]
    cap = max(2, 2 * count // n)
    rows = n * cap
    params = shape_basis.shape[0]
    f32, bf16 = jnp.float32, jnp.bfloat16
    vmem = pl.BlockSpec(memory_space=pltpu.VMEM)
    smem = pl.BlockSpec(memory_space=pltpu.SMEM)
    hbm = pl.BlockSpec(memory_space=pl.ANY)
    x_face = pltpu.VMEM((steps, 2, width_y, depth), f32)
    y_face = pltpu.VMEM((steps, 2, width_x, depth), f32)
    results = pl.pallas_call(
        functools.partial(kernel, grid_x, grid_y),
        out_shape=(
            jax.ShapeDtypeStruct(electric.shape, f32),
            jax.ShapeDtypeStruct(magnetic.shape, f32),
            jax.ShapeDtypeStruct((1, params), f32),
        ),
        in_specs=[vmem, vmem, smem, smem] + [hbm] * 6,
        out_specs=(hbm, hbm, vmem),
        scratch_shapes=[
            pltpu.VMEM(source_values.shape, f32),
            pltpu.VMEM((3, width_x + 1, width_y, depth), f32),
            pltpu.VMEM((3, width_x + 1, width_y, depth), f32),
            pltpu.VMEM(material_ids.shape, jnp.int32),
            pltpu.VMEM(forward_field.shape, bf16),
            pltpu.VMEM((width_x, width_y, params), f32),
            pltpu.VMEM(material_ids.shape, f32),
            pltpu.VMEM(material_ids.shape, f32),
            pltpu.VMEM(material_ids.shape, f32),
            pltpu.VMEM((width_x * width_y, rows), bf16),
            pltpu.VMEM((rows, count), bf16),
            pltpu.VMEM((steps, rows, depth), f32),
            pltpu.VMEM((steps, rows, depth), f32),
            pltpu.VMEM((n, 8, 128), f32),
            pltpu.VMEM((n, 8, 128), f32),
            pltpu.VMEM((rows // 128, 8, 128), jnp.int32),
            pltpu.VMEM((rows, 2 * depth), bf16),
            x_face,
            y_face,
            x_face,
            y_face,
            x_face,
            y_face,
            x_face,
            y_face,
            pltpu.VMEM((8, params), f32),
            pltpu.VMEM((n, 8, params), f32),
            pltpu.SemaphoreType.DMA((6,)),
            pltpu.SemaphoreType.DMA((5,)),
            pltpu.SemaphoreType.DMA((steps + 2,)),
            pltpu.SemaphoreType.DMA((steps + 2,)),
            pltpu.SemaphoreType.DMA((4, steps)),
            pltpu.SemaphoreType.DMA((4, steps)),
        ],
        compiler_params=pltpu.CompilerParams(
            collective_id=0, has_side_effects=True, vmem_limit_bytes=60 * 1024 * 1024
        ),
    )(
        source_tile.reshape(1, count),
        source_cell.reshape(1, count),
        inv_permittivity,
        owner_map,
        source_values,
        electric,
        magnetic,
        material_ids,
        forward_field,
        jnp.transpose(shape_basis, (1, 2, 0)),
    )
    return pl.pallas_call(
        hand_over,
        out_shape=tuple(jax.ShapeDtypeStruct(r.shape, r.dtype) for r in results),
        in_specs=[hbm, hbm, vmem],
        out_specs=(hbm, hbm, vmem),
        scratch_shapes=[
            pltpu.VMEM(electric.shape, f32),
            pltpu.VMEM(magnetic.shape, f32),
            pltpu.SemaphoreType.DMA((2, 3, 4)),
            pltpu.SemaphoreType.DMA((2, 3, 4)),
        ],
        compiler_params=pltpu.CompilerParams(vmem_limit_bytes=60 * 1024 * 1024),
    )(*results)


def solution(mesh):
    placed = (
        P(None, "gx", "gy", None),
        P(None, "gx", "gy", None),
        P("gx", "gy", None),
        P(),
        P(None, None, "gx", "gy", None),
        P(("gx", "gy"), None),
        P(("gx", "gy"), None),
        P(("gx", "gy")),
        P(),
        P(),
    )
    return jax.shard_map(
        per_device,
        mesh=mesh,
        in_specs=placed,
        out_specs=(P(None, "gx", "gy", None), P(None, "gx", "gy", None), P(("gx", "gy"), None)),
        check_vma=False,
    )
```
